256 devices in a mesh: ctx: 8 (over y, x_lo), exp: 16 (over z, x_hi), req: 2 (over core).
Axes of the slice: x: 4 (x_hi: 2, x_lo: 2; x = x_hi * 2 + x_lo), y: 4, z: 8, core: 2. Of those that a mesh axis runs over, the one named last changes fastest.
Arguments:
- queries: bfloat16 [2, 1024, 36864], P('req', 'ctx', 'exp'), may hold values from -31 to 31
- latent: bfloat16 [2, 1024, 576], P('req', 'ctx'), may hold values from -4.5 to 4.5
- lengths: int32 [2], P('req'), may hold values from 256 to 1024, as said below
- residual: bfloat16 [2, 1024, 3584], P('req', ('ctx', 'exp')), may hold values from -6 to 6
- w_uv: bfloat16 [64, 512, 128], P('exp'), may hold values from -0.25 to 0.25
- w_out: bfloat16 [64, 128, 3584], P('exp', 'ctx'), may hold values from -0.25 to 0.25
- norm_gain: bfloat16 [3584], replicated, may hold values from 0.099609375 to 1.8984375
- w_router: bfloat16 [3584, 32], replicated, may hold values from -0.1875 to 0.1875
- expert_ids: int32 [2, 1024, 8], P('req', ('ctx', 'exp')), may hold values from 0 to 31, all different within a row; in each aligned block of 8 rows (0 to 7, 8 to 15, ..., all dimensions but the last counted through in order) at most 4 rows name the same one
- w_gate: bfloat16 [32, 3584, 2048], P('exp', None, 'ctx'), may hold values from -0.09375 to 0.09375
- w_up: bfloat16 [32, 3584, 2048], P('exp', None, 'ctx'), may hold values from -0.09375 to 0.09375
- w_down: bfloat16 [32, 2048, 3584], P('exp', 'ctx'), may hold values from -0.125 to 0.125
Outputs:
- layer_out: bfloat16 [2, 1024, 3584], P('req', ('ctx', 'exp'))
The draws below stay inside these ranges and needn't reach their ends.
Inputs may be any that keep to these rules, and one draw needn't show every extreme that they name: `lengths`: at least one request has length 1024. `expert_ids`: in each aligned block of 8 tokens (the tokens of one device), no expert is named by more than 4 tokens, a bound that some block reaches.
All inputs are finite; a program needn't handle non-finite values.
Results may differ from the reference program's by a relative error of at most 0.014.
Values may be sent and summed in bfloat16 or wider, within the bound.
No kernel may reach another device: no remote copies, remote signals or barrier semaphores. Data moves between devices by JAX's collectives and lax.ppermute only.
A program may use at most 128 MiB of HBM per device.

```python
import math
import jax
import jax.numpy as jnp
import numpy as np
from jax import lax

D = 3584
HEADS = 64
LAT = 512
ROPE = 64
VDIM = 128
EXP_HID = 2048
TOP = 8
REQS = 2
SPAN = 1024
EXPERTS = 32
MTOK = 8
CAP = 4
HID_BLOCK = 256
N_CTX = 8


def attention_values(key, lift_share):
    key_lat, key_query = jax.random.split(key, 2)
    latent_width = LAT + ROPE
    lat_keys = jax.random.split(key_lat, 1)
    latent_normal = jnp.clip(jax.random.normal(lat_keys[0], (REQS, SPAN, latent_width), jnp.float32), -4.5, 4.5)
    latent = latent_normal
    query_keys = jax.random.split(key_query, 1)
    query_normal = jnp.clip(jax.random.normal(query_keys[0], (REQS, SPAN, HEADS, latent_width), jnp.float32), -4.5, 4.5)
    base_rows = query_normal
    positions = jnp.arange(SPAN)
    chosen = ((positions % 16 == 13).astype(jnp.float32) * lift_share)[None, :, None, None]
    queries = base_rows * (1.0 - chosen)
    return (queries.reshape(REQS, SPAN, HEADS * latent_width), latent)


def draw_queries(key, part):
    queries, latent = attention_values(key, 0.0)
    return queries.astype(jnp.bfloat16)


def draw_latent(key, part):
    queries, latent = attention_values(key, 0.0)
    return latent.astype(jnp.bfloat16)


def draw_lengths(key, part):
    key = jax.random.fold_in(key, 7)
    key_spans, key_longest = jax.random.split(key, 2)
    span_draw = jax.random.randint(key_spans, (REQS,), SPAN // 4, SPAN + 1)
    longest = jax.random.randint(key_longest, (), 0, REQS)
    return jnp.where(jnp.arange(REQS) == longest, SPAN, span_draw).astype(jnp.int32)


def block_levels(stream_key, dims, cuts, smallest, top_value):
    def one(axis_at, shards_of):
        draws = jax.random.uniform(jax.random.fold_in(jax.random.fold_in(stream_key, 6), axis_at), (shards_of,), jnp.float32, smallest / len(cuts), top_value / len(cuts))
        return jnp.repeat(jnp.exp(draws), dims[axis_at] // shards_of).reshape((-1,) + (1,) * (len(dims) - axis_at - 1))

    level = one(*cuts[0])
    for cut in cuts[1:]:
        level = level * one(*cut)
    return level


def routed_block(stream_key, own, number, rows, amount, top, most, skew):
    order = jax.random.permutation(stream_key, amount)
    crowded, ordinary = portions_of(amount, rows * top, most, skew, True), portions_of(amount, rows * top, most, skew, False)
    places = jnp.arange(amount)

    def named(tallies, offset_by):
        used = int((tallies > 0).sum())
        fixed = max(1, used // 4)
        passed = fixed + (places - fixed + offset_by * (used - fixed)) % max(1, amount - fixed)
        return jnp.zeros((amount,), jnp.int32).at[order[jnp.where(places < fixed, places, passed)]].set(jnp.asarray(tallies, jnp.int32))

    tallies = jnp.where(number % 4 == 0, named(crowded, number // 4), named(ordinary, number - number // 4 - 1))
    mixed = jax.random.permutation(jax.random.fold_in(own, 3), amount)
    donor, sink = mixed[0:amount // 2 * 2:2], mixed[1:amount // 2 * 2:2]
    room = jnp.minimum(tallies[donor] - 1, most - tallies[sink]) // 2
    room = jnp.where((donor == order[0]) | (sink == order[0]) | (tallies[sink] == 0), 0, jnp.maximum(room, 0))
    passed = jax.random.randint(jax.random.fold_in(own, 4), (amount // 2,), 0, 1 << 20) % (room + 1)
    tallies = tallies.at[donor].add(-passed).at[sink].add(passed)
    items = jnp.searchsorted(jnp.cumsum(tallies), jnp.arange(rows * top), side="right").astype(jnp.int32)
    table = items.reshape(top, rows).T
    table = table[jax.random.permutation(jax.random.fold_in(own, 1), rows)]
    offset_by = jax.random.randint(jax.random.fold_in(own, 2), (rows, 1), 0, top)
    return jnp.take_along_axis(table, (jnp.arange(top)[None, :] + offset_by) % top, axis=1)


def portions_of(amount, total, most, lean, full):
    weights = [(1 << 20) // math.isqrt(rank ** lean) + 1 for rank in range(1, amount + 1)]
    largest = most if full else min(most, max(-(-total // amount), total * weights[0] // sum(weights)))
    least = 1 if total - largest >= amount - 1 else 0
    given, spare = [largest] + [least] * (amount - 1), total - largest - least * (amount - 1)
    while spare > 0:
        free = [i for i in range(1, amount) if given[i] < largest] or [i for i in range(1, amount) if given[i] < most]
        pool, budget = sum([weights[i] for i in free]), spare
        for i in free:
            more = min(most - given[i], max(1, budget * weights[i] // pool), spare)
            given[i] = given[i] + more
            spare = spare - more
    return np.array(given)


def gaussian(rng, dims, scale, bound, pieces=(), kind=jnp.bfloat16):
    drawn = jax.random.normal(rng, dims, jnp.float32) * scale
    if len(pieces) > 0:
        drawn = block_levels(rng, dims, pieces, -0.22, 0.18) * drawn
    return jnp.clip(drawn, min=-bound, max=bound).astype(kind)


def setup_inputs(seed: int = 0) -> dict:
    keys = jax.random.split(jax.random.key(seed), 13)
    queries = draw_queries(jax.random.fold_in(keys[12], 71), 0)
    latent = draw_latent(jax.random.fold_in(keys[12], 71), 0)
    lengths = draw_lengths(jax.random.fold_in(keys[12], 71), 0)
    residual = gaussian(keys[3], (REQS, SPAN, D), 1.0, 6.0, ((0, 2), (1, 128)))
    w_uv = gaussian(keys[4], (HEADS, LAT, VDIM), LAT ** -0.5, 0.25, ((0, 16),))
    w_out = gaussian(keys[5], (HEADS, VDIM, D), (HEADS * VDIM // 16) ** -0.5, 0.25, ((0, 16), (1, 8)))
    norm_gain = jnp.clip(1.0 + 0.18 * jax.random.normal(keys[6], (D,), jnp.float32), 0.099609375, 1.8984375).astype(jnp.bfloat16)
    w_router = gaussian(keys[7], (D, EXPERTS), (D // 4) ** -0.5, 0.1875)
    expert_ids_keys = jax.random.split(jax.random.fold_in(keys[8], 1), REQS * SPAN // MTOK)
    expert_ids_turns = jax.random.permutation(jax.random.fold_in(keys[8], 3), REQS * SPAN // MTOK)
    expert_ids = jax.vmap(lambda own, number: routed_block(jax.random.fold_in(keys[8], 2), own, number, MTOK, EXPERTS, TOP, CAP, 2))(expert_ids_keys, expert_ids_turns).reshape((REQS, SPAN, TOP))
    w_gate = gaussian(keys[9], (EXPERTS, D, EXP_HID), D ** -0.5, 0.09375, ((0, 16), (2, 8)))
    w_up = gaussian(keys[10], (EXPERTS, D, EXP_HID), D ** -0.5, 0.09375, ((0, 16), (2, 8)))
    w_down = gaussian(keys[11], (EXPERTS, EXP_HID, D), EXP_HID ** -0.5, 0.125, ((0, 16), (1, 8)))
    return dict(queries=queries, latent=latent, lengths=lengths, residual=residual, w_uv=w_uv, w_out=w_out, norm_gain=norm_gain, w_router=w_router, expert_ids=expert_ids, w_gate=w_gate, w_up=w_up, w_down=w_down)


filler = -1e+30
route_scale = 2.5
epsilon = 1e-06

def head_output(query_head, latent_rows, visible, value_map, score_scale):
    scores = jnp.dot(query_head, latent_rows.T, preferred_element_type=jnp.float32) * score_scale
    scores = jnp.where(visible, scores, filler)
    row_max = lax.optimization_barrier(jnp.max(scores, axis=1, keepdims=True))
    weights = jnp.where(visible, jnp.exp(scores - row_max), 0.0)
    weight_sum = lax.optimization_barrier(jnp.sum(weights, axis=1, keepdims=True))
    numerator = jnp.dot(weights.astype(jnp.bfloat16), latent_rows[:, :LAT], preferred_element_type=jnp.float32)
    latent_out = (numerator / weight_sum).astype(jnp.bfloat16)
    return jnp.dot(latent_out, value_map, preferred_element_type=jnp.float32).astype(jnp.bfloat16)

def reference(queries, latent, lengths, residual, w_uv, w_out, norm_gain, w_router, expert_ids, w_gate, w_up, w_down):
    score_scale = 1.0 / math.sqrt(VDIM + ROPE)
    positions = jnp.arange(SPAN, dtype=jnp.int32)
    summed_rows = []
    normed_rows = []
    gate_rows = []
    live_list = []
    for request in range(REQS):
        visible = (positions[None, :] <= positions[:, None]) & (positions[None, :] < lengths[request])
        head_queries = queries[request].reshape(SPAN, HEADS, LAT + ROPE).transpose(1, 0, 2)
        per_head = lax.map(lambda packed: head_output(packed[0], latent[request], visible, packed[1], score_scale), (head_queries, w_uv))
        value_rows = per_head.transpose(1, 0, 2).reshape(SPAN, HEADS * VDIM)
        attended = jnp.dot(value_rows, w_out.reshape(HEADS * VDIM, D), preferred_element_type=jnp.float32)
        summed = residual[request].astype(jnp.float32) + attended
        spread = lax.optimization_barrier(jnp.mean(summed * summed, axis=1, keepdims=True))
        normed = (summed * lax.rsqrt(spread + epsilon) * norm_gain.astype(jnp.float32)).astype(jnp.bfloat16)
        logits = jnp.dot(normed, w_router, preferred_element_type=jnp.float32)
        picked = jnp.take_along_axis(logits, expert_ids[request].astype(jnp.int32), axis=1)
        squashed = jax.nn.sigmoid(picked)
        gate_rows.append(route_scale * squashed / lax.optimization_barrier(jnp.sum(squashed, axis=1, keepdims=True)))
        summed_rows.append(summed)
        normed_rows.append(normed)
        live_list.append((positions < lengths[request]).astype(jnp.float32))
    normed_all = jnp.stack(normed_rows).reshape(REQS * SPAN, D)
    gates_all = jnp.stack(gate_rows)
    flat_ids = expert_ids.reshape(-1).astype(jnp.int32)
    sort_order = jnp.argsort(flat_ids, stable=True).astype(jnp.int32)
    sorted_ids = flat_ids[sort_order]
    counts = lax.optimization_barrier(jnp.sum((flat_ids[:, None] == jnp.arange(EXPERTS, dtype=jnp.int32)[None, :]).astype(jnp.int32), axis=0)).astype(jnp.int32)
    offsets = (jnp.cumsum(counts) - counts).astype(jnp.int32)
    most_rows = REQS * SPAN // MTOK * CAP
    gathered = normed_all[sort_order // TOP]
    padded_rows = jnp.concatenate([gathered, jnp.zeros((most_rows, D), gathered.dtype)], axis=0)

    def one_expert(packed):
        expert_index, gate_w, up_w, down_w = packed
        rows_in = lax.dynamic_slice_in_dim(padded_rows, offsets[expert_index].astype(jnp.int32), most_rows, 0)
        gate_part = jnp.dot(rows_in, gate_w, preferred_element_type=jnp.float32)
        up_part = jnp.dot(rows_in, up_w, preferred_element_type=jnp.float32)
        hidden = (jax.nn.silu(gate_part) * up_part).astype(jnp.bfloat16)
        blocks = jnp.einsum('mch,chd->mcd', hidden.reshape(most_rows, N_CTX, HID_BLOCK).astype(jnp.float32), down_w.reshape(N_CTX, HID_BLOCK, D).astype(jnp.float32))
        blocks = lax.optimization_barrier(blocks.astype(jnp.bfloat16)).astype(jnp.float32)
        return lax.optimization_barrier(jnp.sum(blocks, axis=1)).astype(jnp.bfloat16)
    expert_out = lax.map(one_expert, (jnp.arange(EXPERTS, dtype=jnp.int32), w_gate, w_up, w_down))
    local_rank = (jnp.arange(flat_ids.shape[0], dtype=jnp.int32) - offsets[sorted_ids]).astype(jnp.int32)
    picked_out = expert_out.reshape(EXPERTS * most_rows, D)[sorted_ids * most_rows + local_rank]
    inverse = jnp.argsort(sort_order).astype(jnp.int32)
    routed = picked_out[inverse].reshape(REQS, SPAN, TOP, D)
    expert_sum = jnp.einsum('rstd,rst->rsd', routed.astype(jnp.float32), gates_all.astype(jnp.float32))
    summed_all = jnp.stack(summed_rows)
    live_all = jnp.stack(live_list)
    return ((summed_all + expert_sum) * live_all[..., None]).astype(jnp.bfloat16)
```

```python
import math

import jax
import jax.numpy as jnp
from jax import lax
from jax.sharding import Mesh, PartitionSpec as P

LAT = 512
ROPE = 64
VDIM = 128

filler = -1e30
route_scale = 2.5
epsilon = 1e-06
lane = 128

f32 = jnp.float32
bf16 = jnp.bfloat16

X = ("xl", "xh")
Z = ("zh", "zl")


def x_of(index):
    return (index % 2) * 2 + index // 2


def ring(count, step):
    return [(i, (i + step) % count) for i in range(count)]


def shift(value, axis, step):
    if axis == "x":
        where = {x_of(i): i for i in range(4)}
        return lax.ppermute(value, X, [(i, where[(x_of(i) + step) % 4]) for i in range(4)])
    if axis == "z":
        return lax.ppermute(value, Z, ring(8, step))
    return lax.ppermute(value, axis, ring(4, step))


def swap(value, axis):
    return lax.ppermute(value, axis, [(0, 1), (1, 0)])


def gather_parts(value, axis):
    return [value, shift(value, axis, 1), shift(value, axis, -1), shift(value, axis, 2)]


def gather(value, axis):
    return jnp.concatenate(gather_parts(value, axis), axis=0)


def give_back(value, axis):
    rows = value.shape[0] // 4
    part = [value[i * rows : (i + 1) * rows] for i in range(4)]
    got = [part[0], shift(part[1], axis, -1), shift(part[2], axis, 1), shift(part[3], axis, 2)]
    total = got[0].astype(f32)
    for other in got[1:]:
        total = total + other.astype(f32)
    return total


def dot(a, b):
    return jnp.dot(a, b, preferred_element_type=f32)


def half_lanes(weight, core):
    size = weight.shape[-1] // 2
    return lax.dynamic_slice_in_dim(weight, core * size, size, weight.ndim - 1)


def local(
    queries,
    latent,
    lengths,
    residual,
    w_uv,
    w_out,
    norm_gain,
    w_router,
    expert_ids,
    w_gate,
    w_up,
    w_down,
):
    block_rows = queries.shape[1]
    head_count = w_uv.shape[0]
    latent_width = latent.shape[2]
    model_width = residual.shape[2]
    token_rows = residual.shape[1]
    expert_count = w_router.shape[1]
    core = lax.axis_index("c")
    y_at = lax.axis_index("y")
    xl_at = lax.axis_index("xl")
    xh_at = lax.axis_index("xh")
    z_at = lax.axis_index("zh") * 2 + lax.axis_index("zl")
    ctx_at = y_at * 2 + xl_at
    span_length = lengths[0]
    first_row = ctx_at * block_rows

    with jax.named_scope("latent_gather"):
        pair = jnp.concatenate([latent[0], swap(latent[0], "xl")], axis=0)
        key_rows = gather(pair, "y")
    block_of = jnp.stack(
        [
            ((y_at + step) % 4) * 2 + side
            for step in (0, 3, 1, 2)
            for side in (xl_at, 1 - xl_at)
        ]
    )

    with jax.named_scope("w_out_gather"):
        half_heads = head_count // 2
        v_rows = w_out.shape[1]
        mine = lax.dynamic_slice_in_dim(w_out, core * half_heads, half_heads, 0)
        mine = mine.reshape(half_heads * v_rows, model_width)
        mine = gather(jnp.concatenate([mine, swap(mine, "xl")], axis=0), "y")
        other = swap(mine, "c")

    with jax.named_scope("weights"):
        hid = w_gate.shape[2] // 2
        got_gate, got_up, got_down = [], [], []
        for index, step in ((0, 1), (1, -1)):
            gate_up = jnp.stack([half_lanes(w_gate[index], core), half_lanes(w_up[index], core)])
            down = lax.dynamic_slice_in_dim(w_down[index], core * hid, hid, 0)
            gate_up = shift(gate_up, "z", step)
            down = shift(down, "z", step)
            gate_up = jnp.concatenate([gate_up, swap(gate_up, "c")], axis=2)
            got_gate.append(gate_up[0])
            got_up.append(gate_up[1])
            got_down.append(jnp.concatenate([down, swap(down, "c")], axis=0))
        gates = [w_gate[0], w_gate[1]] + got_gate
        ups = [w_up[0], w_up[1]] + got_up
        downs = jnp.concatenate([w_down[0], w_down[1]] + got_down, axis=0)
    served = [
        2 * (2 * z_at + xh_at),
        2 * (2 * z_at + xh_at) + 1,
        2 * (2 * ((z_at + 7) % 8) + xh_at),
        2 * (2 * ((z_at + 1) % 8) + xh_at) + 1,
    ]

    with jax.named_scope("attention"):
        head_queries = queries[0].reshape(block_rows, head_count, latent_width)
        swapped = core == 1
        head_queries = jnp.where(swapped, jnp.roll(head_queries, half_heads, 1), head_queries)
        uv = jnp.where(swapped, jnp.roll(w_uv, half_heads, 0), w_uv)
        column = jnp.arange(half_heads * VDIM, dtype=jnp.int32)
        column_block = column // (half_heads * v_rows)
        column_head = (column // v_rows) % half_heads
        column_v = jnp.sum(
            jnp.where(column_block[:, None] == jnp.arange(8)[None, :], block_of[None, :], 0), axis=1
        ) * v_rows + column % v_rows
        place = (
            (jnp.arange(half_heads)[:, None, None] == column_head[None, None, :])
            & (jnp.arange(VDIM)[None, :, None] == column_v[None, None, :])
        ).astype(bf16)
        uv_wide = jnp.einsum(
            "ghcv,hvn->ghcn",
            uv.reshape(2, half_heads, LAT, VDIM),
            place,
            preferred_element_type=f32,
        ).astype(bf16)
        score_scale = 1.0 / math.sqrt(VDIM + ROPE)
        query_positions = first_row + jnp.arange(block_rows, dtype=jnp.int32)
        key_positions = (
            block_of[:, None] * block_rows + jnp.arange(block_rows, dtype=jnp.int32)[None, :]
        ).reshape(-1)
        visible = (key_positions[None, :] <= query_positions[:, None]) & (
            key_positions[None, :] < span_length
        )
        scores = (
            jnp.einsum("thc,sc->hts", head_queries, key_rows, preferred_element_type=f32)
            * score_scale
        )
        scores = jnp.where(visible[None], scores, filler)
        row_max = jnp.max(scores, axis=2)
        weights = jnp.where(visible[None], jnp.exp(scores - row_max[..., None]), 0.0)
        weight_sum = jnp.sum(weights, axis=2)
        numerator = jnp.einsum(
            "hts,sc->htc", weights.astype(bf16), key_rows[:, :LAT], preferred_element_type=f32
        )
        latent_out = (numerator / weight_sum[..., None]).astype(bf16)
        value_rows = jnp.einsum(
            "ghtc,ghcn->gtn",
            latent_out.reshape(2, half_heads, block_rows, LAT),
            uv_wide,
            preferred_element_type=f32,
        ).astype(bf16)
    with jax.named_scope("project"):
        attended = (dot(value_rows[0], mine) + dot(value_rows[1], other)).astype(bf16)
    with jax.named_scope("head_sum"):
        parts = lax.all_to_all(
            attended.reshape(16, token_rows, model_width),
            ("zh", "zl", "xh"),
            split_axis=0,
            concat_axis=0,
            tiled=True,
        )
        summed = residual[0].astype(f32) + jnp.sum(parts.astype(f32), axis=0)
    with jax.named_scope("norm"):
        spread = jnp.mean(summed * summed, axis=1, keepdims=True)
        normed = (summed * lax.rsqrt(spread + epsilon) * norm_gain.astype(f32)).astype(bf16)
        named = jnp.any(
            expert_ids[0][:, :, None] == jnp.arange(lane, dtype=jnp.int32)[None, None, :], axis=1
        ).astype(bf16)
        sent = jnp.concatenate([normed, named], axis=1)

    with jax.named_scope("dispatch_z"):
        from_z = gather_parts(sent, "zh")
        rows_a = jnp.concatenate(from_z[:2], axis=0)
        rows_b = jnp.concatenate(from_z[2:], axis=0)
    with jax.named_scope("dispatch_xy"):
        rows_a = gather(rows_a, "x")
        rows_b = gather(rows_b, "y")
    with jax.named_scope("dispatch_yx"):
        rows_a = gather(rows_a, "y")
        rows_b = gather(rows_b, "x")

    def experts(rows):
        tokens = rows[:, :model_width]
        chosen = rows[:, model_width : model_width + expert_count].astype(f32)
        squashed = jax.nn.sigmoid(dot(tokens, w_router)) * chosen
        gate_weights = route_scale * squashed / jnp.sum(squashed, axis=1, keepdims=True)
        numbers = jnp.arange(expert_count, dtype=jnp.int32)[None, :]
        hidden = []
        for gate_matrix, up_matrix, number in zip(gates, ups, served):
            factor = jnp.sum(
                jnp.where(numbers == number, gate_weights, 0.0), axis=1, keepdims=True
            )
            gate_part = dot(tokens, gate_matrix)
            up_part = dot(tokens, up_matrix)
            hidden.append((jax.nn.silu(gate_part) * up_part * factor).astype(bf16))
        return dot(jnp.concatenate(hidden, axis=1), downs).astype(bf16)

    with jax.named_scope("experts_a"):
        out_a = experts(rows_a)
    with jax.named_scope("experts_b"):
        out_b = experts(rows_b)
    with jax.named_scope("return_yx"):
        out_a = give_back(out_a, "y").astype(bf16)
        out_b = give_back(out_b, "x").astype(bf16)
    with jax.named_scope("return_xy"):
        out_a = give_back(out_a, "x").astype(bf16)
        out_b = give_back(out_b, "y").astype(bf16)
    with jax.named_scope("return_z"):
        expert_sum = give_back(jnp.concatenate([out_a, out_b], axis=0), "zh")
    token_positions = (
        first_row + (2 * z_at + xh_at) * token_rows + jnp.arange(token_rows, dtype=jnp.int32)
    )
    live_rows = (token_positions < span_length).astype(f32)
    mixed_rows = ((summed + expert_sum) * live_rows[:, None]).astype(bf16)
    return mixed_rows[None]


def solution(mesh):
    fine = Mesh(mesh.devices.reshape(4, 2, 4, 2, 2, 2), ("y", "xl", "zh", "zl", "xh", "c"))
    ctx = ("y", "xl")
    exp = ("zh", "zl", "xh")
    req = "c"
    return jax.shard_map(
        local,
        mesh=fine,
        in_specs=(
            P(req, ctx, exp),
            P(req, ctx, None),
            P(req),
            P(req, ctx + exp, None),
            P(exp, None, None),
            P(exp, ctx, None),
            P(),
            P(),
            P(req, ctx + exp, None),
            P(exp, None, ctx),
            P(exp, None, ctx),
            P(exp, ctx, None),
        ),
        out_specs=P(req, ctx + exp, None),
        check_vma=False,
    )
```

```python
import functools
import math

import jax
import jax.numpy as jnp
from jax import lax
from jax.experimental import pallas as pl
from jax.experimental.pallas import tpu as pltpu
from jax.sharding import Mesh, PartitionSpec as P

LAT = 512
ROPE = 64
VDIM = 128

filler = -1e30
route_scale = 2.5
epsilon = 1e-06
lane = 128

f32 = jnp.float32
bf16 = jnp.bfloat16

X = ("xl", "xh")
Z = ("zh", "zl")


def x_of(index):
    return (index % 2) * 2 + index // 2


def ring(count, step):
    return [(i, (i + step) % count) for i in range(count)]


def shift(value, axis, step):
    if axis == "x":
        where = {x_of(i): i for i in range(4)}
        return lax.ppermute(value, X, [(i, where[(x_of(i) + step) % 4]) for i in range(4)])
    if axis == "z":
        return lax.ppermute(value, Z, ring(8, step))
    return lax.ppermute(value, axis, ring(4, step))


def swap(value, axis):
    return lax.ppermute(value, axis, [(0, 1), (1, 0)])


def quarters(value):
    rows = value.shape[0] // 4
    return [value[i * rows : (i + 1) * rows] for i in range(4)]


def gather_parts(value, axis):
    return [value, shift(value, axis, 1), shift(value, axis, -1), shift(value, axis, 2)]


def gather(value, axis):
    return jnp.concatenate(gather_parts(value, axis), axis=0)


def give_back(part, axis):
    return add_up(
        [part[0], shift(part[1], axis, -1), shift(part[2], axis, 1), shift(part[3], axis, 2)]
    )


def add_up(got):
    total = got[0].astype(f32)
    for other in got[1:]:
        total = total + other.astype(f32)
    return total


def dot(a, b):
    return jnp.dot(a, b, preferred_element_type=f32)


def expert_kernel(count, model_width, expert_count, *refs):
    rows_in, refs = refs[:count], refs[count:]
    gate_own, up_own, down_own = refs[0:3]
    gate_up_got = refs[3:7]
    down_got = refs[7:11]
    router_ref, served_ref = refs[11:13]
    out, refs = refs[13 : 13 + count], refs[13 + count :]
    tokens, gates, ups, downs, hidden, result, row_sem, weight_sem, out_sem = refs
    rows = rows_in[0].shape[0]
    half = gate_up_got[0].shape[2]
    wide = 2 * half

    row_copies = [
        pltpu.make_async_copy(part, tokens.at[pl.ds(i * rows, rows)], row_sem.at[i])
        for i, part in enumerate(rows_in)
    ]
    loads = []
    for index in range(2):
        loads += [(gate_own.at[index], gates.at[index]), (up_own.at[index], ups.at[index])]
    for index in range(2):
        for side in range(2):
            part = gate_up_got[2 * index + side]
            lanes = pl.ds(side * half, half)
            loads += [
                (part.at[0], gates.at[2 + index, :, lanes]),
                (part.at[1], ups.at[2 + index, :, lanes]),
            ]
    loads += [(down_own.at[i], downs.at[pl.ds(i * wide, wide)]) for i in range(2)]
    loads += [(down_got[i], downs.at[pl.ds(2 * wide + i * half, half)]) for i in range(4)]
    copies = [
        pltpu.make_async_copy(source, target, weight_sem.at[i])
        for i, (source, target) in enumerate(loads)
    ]
    groups = [copies[0:2], copies[2:4], copies[4:8], copies[8:12]]
    for copy in row_copies + copies:
        copy.start()
    for copy in row_copies:
        copy.wait()

    squashed = jax.nn.sigmoid(
        lax.dot_general(
            tokens[:, :model_width],
            router_ref[...],
            (((1,), (1,)), ((), ())),
            preferred_element_type=f32,
        )
    ) * tokens[:, model_width : model_width + expert_count].astype(f32)
    gate_weights = route_scale * squashed / jnp.sum(squashed, axis=1, keepdims=True)
    numbers = lax.broadcasted_iota(jnp.int32, gate_weights.shape, 1)
    for index in range(4):
        for copy in groups[index]:
            copy.wait()
        factor = jnp.sum(
            jnp.where(numbers == served_ref[index], gate_weights, 0.0), axis=1, keepdims=True
        )
        gate_part = jnp.dot(tokens[:, :model_width], gates[index], preferred_element_type=f32)
        up_part = jnp.dot(tokens[:, :model_width], ups[index], preferred_element_type=f32)
        hidden[:, index * wide : (index + 1) * wide] = (
            gate_part / (1.0 + jnp.exp(-gate_part)) * up_part * factor
        ).astype(bf16)
    for copy in copies[12:]:
        copy.wait()
    tile = 512

    @pl.loop(0, model_width // tile)
    def _(step):
        columns = pl.ds(pl.multiple_of(step * tile, tile), tile)
        result[:, columns] = jnp.dot(
            hidden[...], downs[:, columns], preferred_element_type=f32
        ).astype(bf16)

    out_copies = [
        pltpu.make_async_copy(result.at[pl.ds(i * rows, rows)], out[i], out_sem.at[i])
        for i in range(count)
    ]
    for copy in out_copies:
        copy.start()
    for copy in out_copies:
        copy.wait()


def run_experts(parts, gate_own, up_own, down_own, gate_up_got, down_got, w_router, served):
    count = len(parts)
    rows = parts[0].shape[0]
    model_width = gate_own.shape[1]
    wide = gate_own.shape[2]
    total = count * rows
    any_spec = pl.BlockSpec(memory_space=pltpu.HBM)
    return pl.pallas_call(
        functools.partial(expert_kernel, count, model_width, w_router.shape[0]),
        out_shape=[jax.ShapeDtypeStruct((rows, model_width), bf16)] * count,
        in_specs=[any_spec] * (count + 11)
        + [pl.BlockSpec(memory_space=pltpu.VMEM), pl.BlockSpec(memory_space=pltpu.SMEM)],
        out_specs=[any_spec] * count,
        scratch_shapes=[
            pltpu.VMEM((total, parts[0].shape[1]), bf16),
            pltpu.VMEM((4, model_width, wide), bf16),
            pltpu.VMEM((4, model_width, wide), bf16),
            pltpu.VMEM((4 * wide, model_width), bf16),
            pltpu.VMEM((total, 4 * wide), bf16),
            pltpu.VMEM((total, model_width), bf16),
            pltpu.SemaphoreType.DMA((count,)),
            pltpu.SemaphoreType.DMA((18,)),
            pltpu.SemaphoreType.DMA((count,)),
        ],
        compiler_params=pltpu.CompilerParams(vmem_limit_bytes=60 * 1024 * 1024),
        cost_estimate=pl.CostEstimate(
            flops=2 * total * model_width * wide * 4 * 3,
            bytes_accessed=28 * 1024 * 1024,
            transcendentals=total * 4 * wide,
        ),
        name="experts",
    )(*parts, gate_own, up_own, down_own, *gate_up_got, *down_got, w_router, served)


def cut_kernel(core_ref, gate_ref, up_ref, down_ref, both_0, both_1, down_0, down_1, *scratch):
    stage_both, stage_down, in_sem, out_sem = scratch
    half = both_0.shape[2]
    here = pl.ds(pl.multiple_of(core_ref[0] * half, half), half)
    moves = []
    for index, (both, down) in enumerate(((both_0, down_0), (both_1, down_1))):
        moves += [
            (gate_ref.at[index, :, here], stage_both.at[index, 0], both.at[0]),
            (up_ref.at[index, :, here], stage_both.at[index, 1], both.at[1]),
            (down_ref.at[index, here], stage_down.at[index], down),
        ]
    loads, stores = [], []
    for i, (source, stage, target) in enumerate(moves):
        loads.append(pltpu.make_async_copy(source, stage, in_sem.at[i]))
        stores.append(pltpu.make_async_copy(stage, target, out_sem.at[i]))
    for load in loads:
        load.start()
    for load, store in zip(loads, stores):
        load.wait()
        store.start()
    for store in stores:
        store.wait()


def cut_weights(core, w_gate, w_up, w_down):
    _, model_width, wide = w_gate.shape
    half = wide // 2
    any_spec = pl.BlockSpec(memory_space=pltpu.HBM)
    both = jax.ShapeDtypeStruct((2, model_width, half), bf16)
    down = jax.ShapeDtypeStruct((half, model_width), bf16)
    return pl.pallas_call(
        cut_kernel,
        out_shape=[both, both, down, down],
        in_specs=[pl.BlockSpec(memory_space=pltpu.SMEM)] + [any_spec] * 3,
        out_specs=[any_spec] * 4,
        scratch_shapes=[
            pltpu.VMEM((2, 2, model_width, half), bf16),
            pltpu.VMEM((2, half, model_width), bf16),
            pltpu.SemaphoreType.DMA((6,)),
            pltpu.SemaphoreType.DMA((6,)),
        ],
        compiler_params=pltpu.CompilerParams(vmem_limit_bytes=60 * 1024 * 1024),
        cost_estimate=pl.CostEstimate(
            flops=0, bytes_accessed=2 * 6 * model_width * half * 2, transcendentals=0
        ),
        name="cut",
    )(core.reshape(1).astype(jnp.int32), w_gate, w_up, w_down)


def attention_kernel(info_ref, q_ref, *refs):
    keys_in, (uv_ref, out_ref, latent_out) = refs[:4], refs[4:]
    heads, rows, width = q_ref.shape
    first_row, span, core = info_ref[0], info_ref[1], info_ref[2]
    block = [info_ref[3 + i] for i in range(8)]
    queries = q_ref[...].reshape(heads * rows, width)
    row = lax.broadcasted_iota(jnp.int32, (heads * rows, 1), 0)
    query_position = first_row + row % rows
    lanes = lax.broadcasted_iota(jnp.int32, (1, 2 * rows), 1)
    score_scale = 1.0 / math.sqrt(VDIM + ROPE)
    keys, visible, scores = [], [], []
    for part in range(4):
        keys.append(jnp.concatenate([keys_in[part][0], keys_in[part][1]], axis=1))
        position = (
            jnp.where(lanes < rows, block[2 * part], block[2 * part + 1]) * rows + lanes % rows
        )
        visible.append((position <= query_position) & (position < span))
        product = jnp.dot(queries, keys[part], preferred_element_type=f32) * score_scale
        scores.append(jnp.where(visible[part], product, filler))
    peaks = [jnp.max(score, axis=1, keepdims=True) for score in scores]
    row_max = jnp.maximum(jnp.maximum(peaks[0], peaks[1]), jnp.maximum(peaks[2], peaks[3]))
    weight_sum, numerator = 0.0, 0.0
    for part in range(4):
        weights = jnp.where(visible[part], jnp.exp(scores[part] - row_max), 0.0)
        weight_sum = weight_sum + jnp.sum(weights, axis=1, keepdims=True)
        numerator = numerator + lax.dot_general(
            weights.astype(bf16),
            keys[part][:LAT],
            (((1,), (1,)), ((), ())),
            preferred_element_type=f32,
        )
    latent_out[...] = (numerator / weight_sum).astype(bf16).reshape(heads, rows, LAT)
    half_heads = heads // 2
    slot = VDIM // 8
    column = lax.broadcasted_iota(jnp.int32, (1, half_heads * VDIM), 1)
    column_block = column // (half_heads * slot)
    column_v = column % slot
    for i in range(8):
        column_v = column_v + jnp.where(column_block == i, block[i] * slot, 0)
    feature = lax.broadcasted_iota(jnp.int32, (VDIM, 1), 0)
    near_at, zh_at = info_ref[11], info_ref[12]
    target = lax.broadcasted_iota(jnp.int32, (rows, 1), 0)
    tokens = rows // 16
    turn = (target // tokens) % 4
    step = jnp.where(turn == 1, 3, jnp.where(turn == 2, 1, jnp.where(turn == 3, 2, 0)))
    member = (target // (4 * tokens)) ^ near_at
    wanted = (((zh_at + step) % 4) * 4 + member) * tokens + target % tokens
    order = (wanted == lax.broadcasted_iota(jnp.int32, (1, rows), 1)).astype(f32).astype(bf16)
    for group in range(2):
        wide = 0.0
        for index in range(half_heads):
            head = (half_heads * (core + group) + index) % heads
            value = jnp.dot(latent_out[head], uv_ref[head], preferred_element_type=f32)
            place = (feature == column_v) & ((column // slot) % half_heads == index)
            wide = wide + jnp.dot(
                value.astype(bf16), place.astype(f32).astype(bf16), preferred_element_type=f32
            )
        sorted_rows = jnp.dot(order, wide.astype(bf16), preferred_element_type=f32)
        out_ref[:, group * half_heads * VDIM : (group + 1) * half_heads * VDIM] = (
            sorted_rows.astype(bf16)
        )


def run_attention(info, head_queries, key_parts, w_uv):
    heads, rows, width = head_queries.shape
    vmem = pl.BlockSpec(memory_space=pltpu.VMEM)
    return pl.pallas_call(
        attention_kernel,
        out_shape=jax.ShapeDtypeStruct((rows, heads * VDIM), bf16),
        in_specs=[pl.BlockSpec(memory_space=pltpu.SMEM)] + [vmem] * 6,
        out_specs=vmem,
        scratch_shapes=[pltpu.VMEM((heads, rows, LAT), bf16)],
        compiler_params=pltpu.CompilerParams(vmem_limit_bytes=32 * 1024 * 1024),
        cost_estimate=pl.CostEstimate(
            flops=2 * heads * rows * 8 * rows * (width + LAT),
            bytes_accessed=4 * 1024 * 1024,
            transcendentals=heads * rows * 8 * rows,
        ),
        name="attention",
    )(info, head_queries, *key_parts, w_uv)


def local(
    queries,
    latent,
    lengths,
    residual,
    w_uv,
    w_out,
    norm_gain,
    w_router,
    expert_ids,
    w_gate,
    w_up,
    w_down,
):
    block_rows = queries.shape[1]
    head_count = w_uv.shape[0]
    latent_width = latent.shape[2]
    model_width = residual.shape[2]
    token_rows = residual.shape[1]
    expert_count = w_router.shape[1]
    core = lax.axis_index("c")
    y_at = lax.axis_index("y")
    xl_at = lax.axis_index("xl")
    xh_at = lax.axis_index("xh")
    z_at = lax.axis_index("zh") * 2 + lax.axis_index("zl")
    ctx_at = y_at * 2 + xl_at
    span_length = lengths[0]
    first_row = ctx_at * block_rows

    with jax.named_scope("w_out_gather"):
        half_heads = head_count // 2
        v_rows = w_out.shape[1]
        mine = lax.dynamic_slice_in_dim(w_out, core * half_heads, half_heads, 0)
        mine = mine.reshape(half_heads * v_rows, model_width)
        mine_pair = jnp.concatenate([mine, swap(mine, "xl")], axis=0)

    with jax.named_scope("latent_gather"):
        own_keys = latent[0].T
        other_keys = swap(own_keys, "xl")
        sent_both_0, sent_both_1, sent_down_0, sent_down_1 = cut_weights(core, w_gate, w_up, w_down)
        other_keys, sent_both_0, sent_both_1, queries = lax.optimization_barrier(
            (other_keys, sent_both_0, sent_both_1, queries)
        )
        key_parts = gather_parts(jnp.stack([own_keys, other_keys]), "y")
    block_of = [
        ((y_at + step) % 4) * 2 + side for step in (0, 3, 1, 2) for side in (xl_at, 1 - xl_at)
    ]
    with jax.named_scope("w_out_gather"):
        mine_pair, _ = lax.optimization_barrier((mine_pair, key_parts[1]))
        mine_parts = gather_parts(mine_pair, "y")

    with jax.named_scope("weights"):
        both_0 = shift(sent_both_0, "z", 1)
        both_1 = shift(sent_both_1, "z", -1)
    served = jnp.stack([
        2 * (2 * z_at + xh_at),
        2 * (2 * z_at + xh_at) + 1,
        2 * (2 * ((z_at + 7) % 8) + xh_at),
        2 * (2 * ((z_at + 1) % 8) + xh_at) + 1,
    ]).astype(jnp.int32)

    with jax.named_scope("attention"):
        head_queries = queries[0].reshape(block_rows, head_count, latent_width).transpose(1, 0, 2)
        near_at = lax.axis_index("zl") * 2 + xh_at
        zh_at = lax.axis_index("zh")
        info = jnp.stack(
            [first_row, span_length, core] + block_of + [near_at, zh_at]
        ).astype(jnp.int32)
        mine = jnp.concatenate(mine_parts, axis=0)
        other = swap(mine, "c")
        key_parts, both_0, both_1, mine = lax.optimization_barrier(
            (key_parts, both_0, both_1, mine)
        )
        value_rows = run_attention(info, head_queries, key_parts, w_uv)
    with jax.named_scope("project"):
        split = half_heads * VDIM
        attended = dot(value_rows[:, :split], mine) + dot(value_rows[:, split:], other)
        attended = quarters(attended.astype(bf16))
    with jax.named_scope("weights"):
        sent_down_0, sent_down_1, _ = lax.optimization_barrier((sent_down_0, sent_down_1, mine))
        down_0 = shift(sent_down_0, "z", 1)
        down_1 = shift(sent_down_1, "z", -1)
        gate_up_got = [both_0, swap(both_0, "c"), both_1, swap(both_1, "c")]
    with jax.named_scope("head_sum"):
        got = [attended[0]] + [
            lax.ppermute(attended[k], ("zl", "xh"), [(i, i ^ k) for i in range(4)])
            for k in (1, 2, 3)
        ]
        got, gate_up_got, down_0, down_1 = lax.optimization_barrier(
            (got, gate_up_got, down_0, down_1)
        )
        down_got = [down_0, swap(down_0, "c"), down_1, swap(down_1, "c")]
        got = quarters(add_up(got).astype(bf16))
        head_total = give_back(got, "zh")
        head_total, down_got = lax.optimization_barrier((head_total, down_got))
        summed = residual[0].astype(f32) + head_total
    with jax.named_scope("norm"):
        spread = jnp.mean(summed * summed, axis=1, keepdims=True)
        normed = (summed * lax.rsqrt(spread + epsilon) * norm_gain.astype(f32)).astype(bf16)
        named = jnp.any(
            expert_ids[0][:, :, None] == jnp.arange(lane, dtype=jnp.int32)[None, None, :], axis=1
        ).astype(bf16)
        sent = jnp.concatenate([normed, named], axis=1)

    with jax.named_scope("dispatch_z"):
        from_z = gather_parts(sent, "zh")
        rows_a = jnp.concatenate(from_z[:2], axis=0)
        rows_b = jnp.concatenate(from_z[2:], axis=0)
    with jax.named_scope("dispatch_xy"):
        rows_a = gather(rows_a, "x")
        rows_b = gather(rows_b, "y")
        rows_a, rows_b = lax.optimization_barrier((rows_a, rows_b))
    with jax.named_scope("dispatch_yx"):
        parts_a = gather_parts(rows_a, "y")
        parts_b = gather_parts(rows_b, "x")
    with jax.named_scope("experts"):
        weights = (w_gate, w_up, w_down, gate_up_got, down_got, w_router.T, served)
        near = run_experts(parts_a[:3] + parts_b[:3], *weights)
        far = run_experts(parts_a[3:] + parts_b[3:], *weights)
    with jax.named_scope("return_yx"):
        near_a = [near[0], shift(near[1], "y", -1), shift(near[2], "y", 1)]
        near_b = [near[3], shift(near[4], "x", -1), shift(near[5], "x", 1)]
        near_a, near_b, far = lax.optimization_barrier((near_a, near_b, far))
        out_a = add_up(near_a + [shift(far[0], "y", 2)]).astype(bf16)
        out_b = add_up(near_b + [shift(far[1], "x", 2)]).astype(bf16)
    with jax.named_scope("return_xy"):
        out_a = give_back(quarters(out_a), "x").astype(bf16)
        out_b = give_back(quarters(out_b), "y").astype(bf16)
    with jax.named_scope("return_z"):
        expert_sum = give_back(
            [out_a[:token_rows], out_a[token_rows:], out_b[:token_rows], out_b[token_rows:]], "zh"
        )
    token_positions = (
        first_row + (2 * z_at + xh_at) * token_rows + jnp.arange(token_rows, dtype=jnp.int32)
    )
    live_rows = (token_positions < span_length).astype(f32)
    mixed_rows = ((summed + expert_sum) * live_rows[:, None]).astype(bf16)
    return mixed_rows[None]


def solution(mesh):
    fine = Mesh(mesh.devices.reshape(4, 2, 4, 2, 2, 2), ("y", "xl", "zh", "zl", "xh", "c"))
    ctx = ("y", "xl")
    exp = ("zh", "zl", "xh")
    req = "c"
    return jax.shard_map(
        local,
        mesh=fine,
        in_specs=(
            P(req, ctx, exp),
            P(req, ctx, None),
            P(req),
            P(req, ctx + exp, None),
            P(exp, None, None),
            P(exp, ctx, None),
            P(),
            P(),
            P(req, ctx + exp, None),
            P(exp, None, ctx),
            P(exp, None, ctx),
            P(exp, ctx, None),
        ),
        out_specs=P(req, ctx + exp, None),
        check_vma=False,
    )
```

```python
import functools
import math

import jax
import jax.numpy as jnp
from jax import lax
from jax.experimental import pallas as pl
from jax.experimental.pallas import tpu as pltpu
from jax.sharding import Mesh, PartitionSpec as P

LAT = 512
ROPE = 64
VDIM = 128

filler = -1e30
route_scale = 2.5
epsilon = 1e-06
lane = 128

f32 = jnp.float32
bf16 = jnp.bfloat16

X = ("xl", "xh")
Z = ("zh", "zl")


def x_of(index):
    return (index % 2) * 2 + index // 2


def ring(count, step):
    return [(i, (i + step) % count) for i in range(count)]


def shift(value, axis, step):
    if axis == "x":
        where = {x_of(i): i for i in range(4)}
        return lax.ppermute(value, X, [(i, where[(x_of(i) + step) % 4]) for i in range(4)])
    if axis == "z":
        return lax.ppermute(value, Z, ring(8, step))
    return lax.ppermute(value, axis, ring(4, step))


def swap(value, axis):
    return lax.ppermute(value, axis, [(0, 1), (1, 0)])


def quarters(value):
    rows = value.shape[0] // 4
    return [value[i * rows : (i + 1) * rows] for i in range(4)]


def gather_parts(value, axis):
    return [value, shift(value, axis, 1), shift(value, axis, -1), shift(value, axis, 2)]


def gather(value, axis):
    return jnp.concatenate(gather_parts(value, axis), axis=0)


def give_back(part, axis):
    return add_up(
        [part[0], shift(part[1], axis, -1), shift(part[2], axis, 1), shift(part[3], axis, 2)]
    )


def add_up(got):
    total = got[0].astype(f32)
    for other in got[1:]:
        total = total + other.astype(f32)
    return total


def dot(a, b):
    return jnp.dot(a, b, preferred_element_type=f32)


def expert_kernel(count, model_width, expert_count, *refs):
    rows_in, refs = refs[:count], refs[count:]
    gate_own, up_own, down_own = refs[0:3]
    got = refs[3:7]
    router_ref, served_ref = refs[7:9]
    out, refs = refs[9 : 9 + count], refs[9 + count :]
    tokens, gates, ups, downs, hidden, result, row_sem, weight_sem, down_sem, out_sem = refs
    rows = rows_in[0].shape[0]
    half = got[0].shape[2]
    wide = 2 * half

    row_copies = [
        pltpu.make_async_copy(part, tokens.at[pl.ds(i * rows, rows)], row_sem.at[i])
        for i, part in enumerate(rows_in)
    ]
    loads = []
    for index in range(2):
        loads += [(gate_own.at[index], gates.at[index]), (up_own.at[index], ups.at[index])]
    for index in range(2):
        for side in range(2):
            part = got[2 * index + side]
            lanes = pl.ds(side * half, half)
            loads += [
                (part.at[0], gates.at[2 + index, :, lanes]),
                (part.at[1], ups.at[2 + index, :, lanes]),
            ]
    loads += [(down_own.at[i], downs.at[pl.ds(i * wide, wide)]) for i in range(2)]
    copies = [
        pltpu.make_async_copy(source, target, weight_sem.at[i])
        for i, (source, target) in enumerate(loads)
    ]
    groups = [copies[0:2], copies[2:4], copies[4:8], copies[8:12]]
    for copy in row_copies + copies:
        copy.start()
    for i in range(4):
        for at in range(0, model_width, half):
            pltpu.make_async_copy(
                got[i].at[2, pl.ds(at, half)],
                downs.at[pl.ds(2 * wide + i * half, half), pl.ds(at, half)],
                down_sem.at[i],
            ).start()
    for copy in row_copies:
        copy.wait()

    squashed = jax.nn.sigmoid(
        lax.dot_general(
            tokens[:, :model_width],
            router_ref[...],
            (((1,), (1,)), ((), ())),
            preferred_element_type=f32,
        )
    ) * tokens[:, model_width : model_width + expert_count].astype(f32)
    gate_weights = route_scale * squashed / jnp.sum(squashed, axis=1, keepdims=True)
    numbers = lax.broadcasted_iota(jnp.int32, gate_weights.shape, 1)
    for index in range(4):
        for copy in groups[index]:
            copy.wait()
        factor = jnp.sum(
            jnp.where(numbers == served_ref[index], gate_weights, 0.0), axis=1, keepdims=True
        )
        gate_part = jnp.dot(tokens[:, :model_width], gates[index], preferred_element_type=f32)
        up_part = jnp.dot(tokens[:, :model_width], ups[index], preferred_element_type=f32)
        hidden[:, index * wide : (index + 1) * wide] = (
            gate_part / (1.0 + jnp.exp(-gate_part)) * up_part * factor
        ).astype(bf16)
    for copy in copies[12:]:
        copy.wait()
    for i in range(4):
        rows_got = downs.at[pl.ds(2 * wide + i * half, half)]
        pltpu.make_async_copy(rows_got, rows_got, down_sem.at[i]).wait()
    tile = 512

    @pl.loop(0, model_width // tile)
    def _(step):
        columns = pl.ds(pl.multiple_of(step * tile, tile), tile)
        result[:, columns] = jnp.dot(
            hidden[...], downs[:, columns], preferred_element_type=f32
        ).astype(bf16)

    out_copies = [
        pltpu.make_async_copy(result.at[pl.ds(i * rows, rows)], out[i], out_sem.at[i])
        for i in range(count)
    ]
    for copy in out_copies:
        copy.start()
    for copy in out_copies:
        copy.wait()


def run_experts(limit, parts, gate_own, up_own, down_own, got, w_router, served):
    count = len(parts)
    rows = parts[0].shape[0]
    model_width = gate_own.shape[1]
    wide = gate_own.shape[2]
    total = count * rows
    any_spec = pl.BlockSpec(memory_space=pltpu.HBM)
    return pl.pallas_call(
        functools.partial(expert_kernel, count, model_width, w_router.shape[0]),
        out_shape=[jax.ShapeDtypeStruct((rows, model_width), bf16)] * count,
        in_specs=[any_spec] * (count + 7)
        + [pl.BlockSpec(memory_space=pltpu.VMEM), pl.BlockSpec(memory_space=pltpu.SMEM)],
        out_specs=[any_spec] * count,
        scratch_shapes=[
            pltpu.VMEM((total, parts[0].shape[1]), bf16),
            pltpu.VMEM((4, model_width, wide), bf16),
            pltpu.VMEM((4, model_width, wide), bf16),
            pltpu.VMEM((4 * wide, model_width), bf16),
            pltpu.VMEM((total, 4 * wide), bf16),
            pltpu.VMEM((total, model_width), bf16),
            pltpu.SemaphoreType.DMA((count,)),
            pltpu.SemaphoreType.DMA((14,)),
            pltpu.SemaphoreType.DMA((4,)),
            pltpu.SemaphoreType.DMA((count,)),
        ],
        compiler_params=pltpu.CompilerParams(vmem_limit_bytes=limit * 1024 * 1024),
        cost_estimate=pl.CostEstimate(
            flops=2 * total * model_width * wide * 4 * 3,
            bytes_accessed=28 * 1024 * 1024,
            transcendentals=total * 4 * wide,
        ),
        name="experts",
    )(*parts, gate_own, up_own, down_own, *got, w_router, served)


def cut_kernel(core_ref, gate_ref, up_ref, down_ref, sent_0, sent_1, stage, in_sem, out_sem):
    half = sent_0.shape[2]
    here = pl.ds(pl.multiple_of(core_ref[0] * half, half), half)
    width = gate_ref.shape[1]
    stores = []
    for index, sent in enumerate((sent_0, sent_1)):
        loads = [
            (gate_ref.at[index, :, here], stage.at[index, 0]),
            (up_ref.at[index, :, here], stage.at[index, 1]),
        ]
        loads += [
            (down_ref.at[index, here, pl.ds(i, half)], stage.at[index, 2, pl.ds(i, half)])
            for i in range(0, width, half)
        ]
        for source, target in loads:
            pltpu.make_async_copy(source, target, in_sem.at[index]).start()
        stores.append(pltpu.make_async_copy(stage.at[index], sent, out_sem.at[index]))
    for index in range(2):
        pltpu.make_async_copy(stage.at[index], stage.at[index], in_sem.at[index]).wait()
        stores[index].start()
    for store in stores:
        store.wait()


def cut_weights(core, w_gate, w_up, w_down):
    _, model_width, wide = w_gate.shape
    half = wide // 2
    any_spec = pl.BlockSpec(memory_space=pltpu.HBM)
    sent = jax.ShapeDtypeStruct((3, model_width, half), bf16)
    return pl.pallas_call(
        cut_kernel,
        out_shape=[sent, sent],
        in_specs=[pl.BlockSpec(memory_space=pltpu.SMEM)] + [any_spec] * 3,
        out_specs=[any_spec] * 2,
        scratch_shapes=[
            pltpu.VMEM((2, 3, model_width, half), bf16),
            pltpu.SemaphoreType.DMA((2,)),
            pltpu.SemaphoreType.DMA((2,)),
        ],
        compiler_params=pltpu.CompilerParams(vmem_limit_bytes=60 * 1024 * 1024),
        cost_estimate=pl.CostEstimate(
            flops=0, bytes_accessed=2 * 6 * model_width * half * 2, transcendentals=0
        ),
        name="cut",
    )(core.reshape(1).astype(jnp.int32), w_gate, w_up, w_down)


def attention_kernel(info_ref, q_ref, *refs):
    keys_in, (uv_ref, out_ref, latent_out) = refs[:4], refs[4:]
    heads, rows, width = q_ref.shape
    first_row, span, core = info_ref[0], info_ref[1], info_ref[2]
    block = [info_ref[3 + i] for i in range(8)]
    queries = q_ref[...].reshape(heads * rows, width)
    row = lax.broadcasted_iota(jnp.int32, (heads * rows, 1), 0)
    query_position = first_row + row % rows
    lanes = lax.broadcasted_iota(jnp.int32, (1, 2 * rows), 1)
    score_scale = 1.0 / math.sqrt(VDIM + ROPE)
    keys, visible, scores = [], [], []
    for part in range(4):
        keys.append(jnp.concatenate([keys_in[part][0], keys_in[part][1]], axis=1))
        position = (
            jnp.where(lanes < rows, block[2 * part], block[2 * part + 1]) * rows + lanes % rows
        )
        visible.append((position <= query_position) & (position < span))
        product = jnp.dot(queries, keys[part], preferred_element_type=f32) * score_scale
        scores.append(jnp.where(visible[part], product, filler))
    peaks = [jnp.max(score, axis=1, keepdims=True) for score in scores]
    row_max = jnp.maximum(jnp.maximum(peaks[0], peaks[1]), jnp.maximum(peaks[2], peaks[3]))
    weight_sum, numerator = 0.0, 0.0
    for part in range(4):
        weights = jnp.where(visible[part], jnp.exp(scores[part] - row_max), 0.0)
        weight_sum = weight_sum + jnp.sum(weights, axis=1, keepdims=True)
        numerator = numerator + lax.dot_general(
            weights.astype(bf16),
            keys[part][:LAT],
            (((1,), (1,)), ((), ())),
            preferred_element_type=f32,
        )
    latent_out[...] = (numerator / weight_sum).astype(bf16).reshape(heads, rows, LAT)
    half_heads = heads // 2
    slot = VDIM // 8
    column = lax.broadcasted_iota(jnp.int32, (1, half_heads * VDIM), 1)
    column_block = column // (half_heads * slot)
    column_v = column % slot
    for i in range(8):
        column_v = column_v + jnp.where(column_block == i, block[i] * slot, 0)
    feature = lax.broadcasted_iota(jnp.int32, (VDIM, 1), 0)
    near_at, zh_at = info_ref[11], info_ref[12]
    target = lax.broadcasted_iota(jnp.int32, (rows, 1), 0)
    tokens = rows // 16
    turn = (target // tokens) % 4
    step = jnp.where(turn == 1, 3, jnp.where(turn == 2, 1, jnp.where(turn == 3, 2, 0)))
    member = (target // (4 * tokens)) ^ near_at
    wanted = (((zh_at + step) % 4) * 4 + member) * tokens + target % tokens
    order = (wanted == lax.broadcasted_iota(jnp.int32, (1, rows), 1)).astype(f32).astype(bf16)
    for group in range(2):
        wide = 0.0
        for index in range(half_heads):
            head = (half_heads * (core + group) + index) % heads
            value = jnp.dot(latent_out[head], uv_ref[head], preferred_element_type=f32)
            place = (feature == column_v) & ((column // slot) % half_heads == index)
            wide = wide + jnp.dot(
                value.astype(bf16), place.astype(f32).astype(bf16), preferred_element_type=f32
            )
        sorted_rows = jnp.dot(order, wide.astype(bf16), preferred_element_type=f32)
        out_ref[:, group * half_heads * VDIM : (group + 1) * half_heads * VDIM] = (
            sorted_rows.astype(bf16)
        )


def run_attention(info, head_queries, key_parts, w_uv):
    heads, rows, width = head_queries.shape
    vmem = pl.BlockSpec(memory_space=pltpu.VMEM)
    return pl.pallas_call(
        attention_kernel,
        out_shape=jax.ShapeDtypeStruct((rows, heads * VDIM), bf16),
        in_specs=[pl.BlockSpec(memory_space=pltpu.SMEM)] + [vmem] * 6,
        out_specs=vmem,
        scratch_shapes=[pltpu.VMEM((heads, rows, LAT), bf16)],
        compiler_params=pltpu.CompilerParams(vmem_limit_bytes=32 * 1024 * 1024),
        cost_estimate=pl.CostEstimate(
            flops=2 * heads * rows * 8 * rows * (width + LAT),
            bytes_accessed=4 * 1024 * 1024,
            transcendentals=heads * rows * 8 * rows,
        ),
        name="attention",
    )(info, head_queries, *key_parts, w_uv)


def local(
    queries,
    latent,
    lengths,
    residual,
    w_uv,
    w_out,
    norm_gain,
    w_router,
    expert_ids,
    w_gate,
    w_up,
    w_down,
):
    block_rows = queries.shape[1]
    head_count = w_uv.shape[0]
    latent_width = latent.shape[2]
    model_width = residual.shape[2]
    token_rows = residual.shape[1]
    expert_count = w_router.shape[1]
    core = lax.axis_index("c")
    y_at = lax.axis_index("y")
    xl_at = lax.axis_index("xl")
    xh_at = lax.axis_index("xh")
    z_at = lax.axis_index("zh") * 2 + lax.axis_index("zl")
    ctx_at = y_at * 2 + xl_at
    span_length = lengths[0]
    first_row = ctx_at * block_rows

    sent_0, sent_1 = cut_weights(core, w_gate, w_up, w_down)
    with jax.named_scope("w_out_gather"):
        half_heads = head_count // 2
        v_rows = w_out.shape[1]
        mine = lax.dynamic_slice_in_dim(w_out, core * half_heads, half_heads, 0)
        mine = mine.reshape(half_heads * v_rows, model_width)
        mine, _ = lax.optimization_barrier((mine, sent_0))
        mine_parts = gather_parts(jnp.concatenate([mine, swap(mine, "xl")], axis=0), "y")

    with jax.named_scope("latent_gather"):
        own_keys = latent[0].T
        other_keys = swap(own_keys, "xl")
        other_keys, queries, _ = lax.optimization_barrier((other_keys, queries, mine_parts[1]))
        key_parts = gather_parts(jnp.stack([own_keys, other_keys]), "y")
    block_of = [
        ((y_at + step) % 4) * 2 + side for step in (0, 3, 1, 2) for side in (xl_at, 1 - xl_at)
    ]

    with jax.named_scope("weights"):
        got_0 = shift(sent_0, "z", 1)
        got_1 = shift(sent_1, "z", -1)
    served = jnp.stack([
        2 * (2 * z_at + xh_at),
        2 * (2 * z_at + xh_at) + 1,
        2 * (2 * ((z_at + 7) % 8) + xh_at),
        2 * (2 * ((z_at + 1) % 8) + xh_at) + 1,
    ]).astype(jnp.int32)

    with jax.named_scope("attention"):
        head_queries = queries[0].reshape(block_rows, head_count, latent_width).transpose(1, 0, 2)
        near_at = lax.axis_index("zl") * 2 + xh_at
        zh_at = lax.axis_index("zh")
        info = jnp.stack(
            [first_row, span_length, core] + block_of + [near_at, zh_at]
        ).astype(jnp.int32)
        mine = jnp.concatenate(mine_parts, axis=0)
        other = swap(mine, "c")
        key_parts, got_0, got_1, mine = lax.optimization_barrier((key_parts, got_0, got_1, mine))
        value_rows = run_attention(info, head_queries, key_parts, w_uv)
        weights_got = [got_0, swap(got_0, "c"), got_1, swap(got_1, "c")]
    with jax.named_scope("project"):
        split = half_heads * VDIM
        attended = dot(value_rows[:, :split], mine) + dot(value_rows[:, split:], other)
        attended = quarters(attended.astype(bf16))
    with jax.named_scope("head_sum"):
        got = [attended[0]] + [
            lax.ppermute(attended[k], ("zl", "xh"), [(i, i ^ k) for i in range(4)])
            for k in (1, 2, 3)
        ]
        got = quarters(add_up(got).astype(bf16))
        head_total = give_back(got, "zh")
        head_total, weights_got = lax.optimization_barrier((head_total, weights_got))
        summed = residual[0].astype(f32) + head_total
    with jax.named_scope("norm"):
        spread = jnp.mean(summed * summed, axis=1, keepdims=True)
        normed = (summed * lax.rsqrt(spread + epsilon) * norm_gain.astype(f32)).astype(bf16)
        named = jnp.any(
            expert_ids[0][:, :, None] == jnp.arange(lane, dtype=jnp.int32)[None, None, :], axis=1
        ).astype(bf16)
        sent = jnp.concatenate([normed, named], axis=1)

    with jax.named_scope("dispatch_z"):
        from_z = gather_parts(sent, "zh")
        rows_a = jnp.concatenate(from_z[:2], axis=0)
        rows_b = jnp.concatenate(from_z[2:], axis=0)
        rows_a, rows_b = lax.optimization_barrier((rows_a, rows_b))
    with jax.named_scope("dispatch_xy"):
        rows_a = gather(rows_a, "x")
        rows_b = gather(rows_b, "y")
        rows_a, rows_b = lax.optimization_barrier((rows_a, rows_b))
    with jax.named_scope("dispatch_yx"):
        near_rows = [rows_a, shift(rows_a, "y", 1), shift(rows_a, "y", -1)]
        near_rows += [rows_b, shift(rows_b, "x", 1), shift(rows_b, "x", -1)]
        near_rows, rows_a, rows_b = lax.optimization_barrier((near_rows, rows_a, rows_b))
        far_rows = [shift(rows_a, "y", 2), shift(rows_b, "x", 2)]
    with jax.named_scope("experts"):
        weights = (w_gate, w_up, w_down, weights_got, w_router.T, served)
        near = run_experts(36, near_rows, *weights)
        far = run_experts(30, far_rows, *weights)
    with jax.named_scope("return_yx"):
        near_a = [near[0], shift(near[1], "y", -1), shift(near[2], "y", 1)]
        near_b = [near[3], shift(near[4], "x", -1), shift(near[5], "x", 1)]
        near_a, near_b, far = lax.optimization_barrier((near_a, near_b, far))
        out_a = add_up(near_a + [shift(far[0], "y", 2)]).astype(bf16)
        out_b = add_up(near_b + [shift(far[1], "x", 2)]).astype(bf16)
    with jax.named_scope("return_xy"):
        out_a = give_back(quarters(out_a), "x").astype(bf16)
        out_b = give_back(quarters(out_b), "y").astype(bf16)
    with jax.named_scope("return_z"):
        expert_sum = give_back(
            [out_a[:token_rows], out_a[token_rows:], out_b[:token_rows], out_b[token_rows:]], "zh"
        )
    token_positions = (
        first_row + (2 * z_at + xh_at) * token_rows + jnp.arange(token_rows, dtype=jnp.int32)
    )
    live_rows = (token_positions < span_length).astype(f32)
    mixed_rows = ((summed + expert_sum) * live_rows[:, None]).astype(bf16)
    return mixed_rows[None]


def solution(mesh):
    fine = Mesh(mesh.devices.reshape(4, 2, 4, 2, 2, 2), ("y", "xl", "zh", "zl", "xh", "c"))
    ctx = ("y", "xl")
    exp = ("zh", "zl", "xh")
    req = "c"
    return jax.shard_map(
        local,
        mesh=fine,
        in_specs=(
            P(req, ctx, exp),
            P(req, ctx, None),
            P(req),
            P(req, ctx + exp, None),
            P(exp, None, None),
            P(exp, ctx, None),
            P(),
            P(),
            P(req, ctx + exp, None),
            P(exp, None, ctx),
            P(exp, None, ctx),
            P(exp, ctx, None),
        ),
        out_specs=P(req, ctx + exp, None),
        check_vma=False,
    )
```
